1024 devices in a mesh: aux: 16 (over x, y_lo, core), blk: 64 (over y_hi, z).
Axes of the slice: x: 4, y: 8 (y_hi: 4, y_lo: 2; y = y_hi * 2 + y_lo), z: 16, core: 2. Of those that a mesh axis runs over, the one named last changes fastest.
Arguments:
- b_tensor: bfloat16 [64, 16, 256, 128], P('blk', None, 'aux'), may hold values from -2 to 2
- significance: int32 [64, 16, 2], P(None, 'aux'), may hold values from 0 to 1, as said below
- pair_keep: int32 [16, 64, 64], P('aux'), may hold values 0 or 1
- occ_energy: float32 [64, 16], P(None, 'aux'), may hold values from -1.2 to -0.3
- virt_energy: float32 [16, 128], P('aux'), may hold values from 0.3 to 2.5
Outputs:
- gamma: float32 [64, 16, 256, 128], P('blk', None, 'aux')
The draws below stay inside these ranges and needn't reach their ends.
Inputs may be any that keep to these rules, and one draw needn't show every extreme that they name: `significance`: every orbital has at least one significant block among its 2.
All inputs are finite; a program needn't handle non-finite values. No bound on the sum of `pair_keep` on one device may be relied on, other than what follows from the above.
Results may differ from the reference program's by a relative error of at most 0.00062.
Values may be sent and summed in bfloat16 or wider, within the bound.
No kernel may reach another device: no remote copies, remote signals or barrier semaphores. Data moves between devices by JAX's collectives and lax.ppermute only.
A program may use at most 32 MiB of HBM per device.

```python
import jax
import jax.numpy as jnp
from jax import lax

V = 128
ABLK = 128
DOM = 2
DOMA = 256
NRING = 64
NREG = 16


def draw_significance(key, part):
    key = jax.random.fold_in(key, 7)
    first, second = jax.random.split(key)
    bits = jax.random.randint(first, (NRING, NREG, DOM), 0, 2)
    pick = jax.random.randint(second, (NRING, NREG, 1), 0, DOM)
    slots = jnp.arange(DOM, dtype=jnp.int32)[None, None, :]
    forced = (slots == pick).astype(jnp.int32)
    return jnp.maximum(bits, forced).astype(jnp.int32)


def touch_ends(values, stream_key, low, high):
    shape = values.shape
    spot = [jax.random.randint(jax.random.fold_in(stream_key, axis), (), 0, shape[axis]) for axis in range(len(shape))]
    values = values.at[tuple(spot)].set(low)
    longest = shape.index(max(shape))
    spot[longest] = (spot[longest] + 1) % shape[longest]
    return values.at[tuple(spot)].set(high)


def block_scale(key, dims, pieces, smallest, largest):
    gain = 1.0
    for dim, blocks in pieces:
        draws = jax.random.uniform(jax.random.fold_in(jax.random.fold_in(key, 6), dim), (blocks,), jnp.float32, smallest / len(pieces), largest / len(pieces))
        gain = gain * jnp.repeat(jnp.exp(draws), dims[dim] // blocks).reshape((-1,) + (1,) * (len(dims) - 1 - dim))
    return gain


def gaussian(rng, dims, spread, reach, cuts=(), kind=jnp.bfloat16):
    values = jax.random.normal(rng, dims, jnp.float32) * spread
    if len(cuts) > 0:
        values = block_scale(rng, dims, cuts, -0.22, 0.18) * values
    return jnp.clip(values, min=-reach, max=reach).astype(kind)


def setup_inputs(seed: int = 0) -> dict:
    keys = jax.random.split(jax.random.key(seed), 6)
    return {
        "b_tensor": gaussian(keys[0], (NRING, NREG, DOMA, V), 0.15, 2.0, ((0, 64), (2, 16))),
        "significance": draw_significance(jax.random.fold_in(keys[5], 71), 0),
        "pair_keep": touch_ends((jax.random.randint(keys[2], (NREG, NRING, NRING), 0, 4) < 3).astype(jnp.int32), jax.random.fold_in(keys[2], 1), 0, 1),
        "occ_energy": jnp.clip(-1.2 + 0.90000004 * jax.random.uniform(keys[3], (NRING, NREG), jnp.float32) ** block_scale(keys[3], (NRING, NREG), ((1, 16),), -0.2, 0.2), -1.2, -0.3),
        "virt_energy": jnp.clip(0.3 + 2.2 * jax.random.uniform(keys[4], (NREG, V), jnp.float32) ** block_scale(keys[4], (NREG, V), ((0, 16),), -0.2, 0.2), 0.3, 2.5),
    }


def reference(b_tensor, significance, pair_keep, occ_energy, virt_energy):
    mask = jnp.repeat(significance, ABLK, axis=2)
    masked = jnp.where(mask[..., None] > 0, b_tensor, jnp.zeros((), b_tensor.dtype))
    rows = jnp.arange(NRING, dtype=jnp.int32)
    upper = rows[None, :] >= rows[:, None]

    def region(index):
        blocks = masked[:, index].astype(jnp.float32)
        keep = pair_keep[index]
        sym = jnp.where(upper, keep, keep.T).astype(jnp.float32)
        occupied = occ_energy[:, index]
        virtual = virt_energy[index]
        own_mask = mask[:, index].astype(jnp.float32)

        def orbital(place):
            own = blocks[place]
            ints = jnp.einsum('xa,qxb->qab', own, blocks)
            denom = occupied[place] + occupied[:, None, None] - virtual[None, :, None] - virtual[None, None, :]
            amp = sym[place][:, None, None] * ints / denom
            tilde = (2.0 * amp - jnp.swapaxes(amp, 1, 2)).astype(jnp.bfloat16)
            tilde = lax.optimization_barrier(tilde).astype(jnp.float32)
            gam = jnp.einsum('qab,qxb->xa', tilde, blocks)
            return gam * own_mask[place][:, None]

        return lax.map(orbital, rows)

    result = lax.map(region, jnp.arange(NREG, dtype=jnp.int32))
    return jnp.transpose(result, (1, 0, 2, 3))
```

```python
import jax
import jax.numpy as jnp
from jax import lax
from jax.experimental import pallas as pl
from jax.experimental.pallas import tpu as pltpu
from jax.sharding import Mesh, PartitionSpec as P

AUX = ("aux_x", "aux_y", "aux_core")
NP = 4
NH = 4
NL = 4
NZ = NH * NL
NC = NZ // 2
V = 128
AB = 128
NA = 256


def pair_kernel(sig, keep, occ, virt, p_ref, q0, q1, q2a, q2b, q3, out, pcat, pcat_t, qcat, vb, acc):
    h = lax.axis_index("blk_y")
    near = lax.axis_index("blk_near")
    rows = lax.broadcasted_iota(jnp.int32, (NA, V), 0)
    zero = jnp.zeros((NA, V), jnp.bfloat16)

    def masked(block, orbital):
        live = jnp.where(rows < AB, sig[0, orbital], sig[1, orbital]) > 0
        return jnp.where(live, block, zero)

    def q_index(chunk, t):
        far = 2 * lax.rem(chunk, 2) + t
        return h * NZ + far * NL + lax.rem(near + lax.div(chunk, 2), NL)

    w = lax.axis_index("blk_far") * NL + near
    p_index = [s * NZ + w for s in range(NP)]
    for s in range(NP):
        block = masked(p_ref[s], p_index[s])
        pcat[:, s * V : (s + 1) * V] = block
        pcat_t[s * V : (s + 1) * V, :] = block.T
    halves = [(q0, 0), (q0, 2), (q1, 0), (q1, 2), (q2a, 0), (q2b, 0), (q3, 0), (q3, 2)]
    for c, (ref, first) in enumerate(halves):
        for t in range(2):
            qcat[c, :, t * V : (t + 1) * V] = masked(ref[first + t], q_index(c, t))
    va = virt[...]
    vb[...] = jnp.broadcast_to(va, (V, V)).T
    acc[...] = jnp.zeros_like(acc)

    @pl.loop(0, NC)
    def chunk(c):
        block = qcat[c]
        x = jnp.dot(block.T, pcat[...], preferred_element_type=jnp.float32)
        y = jnp.dot(pcat_t[...], block, preferred_element_type=jnp.float32)
        columns = []
        for s in range(NP):
            tiles = []
            for t in range(2):
                p, q = p_index[s], q_index(c, t)
                kept = keep[lax.min(p, q), lax.max(p, q)].astype(jnp.float32)
                total = occ[0, p] + occ[0, q]
                xt = x[t * V : (t + 1) * V, s * V : (s + 1) * V]
                yt = y[s * V : (s + 1) * V, t * V : (t + 1) * V]
                denom = (total - va) - vb[...]
                tiles.append((kept * (2.0 * xt - yt) / denom).astype(jnp.bfloat16))
            columns.append(jnp.concatenate(tiles, axis=0))
        tilde = jnp.concatenate(columns, axis=1)
        acc[...] += jnp.dot(block, tilde, preferred_element_type=jnp.float32)

    for s in range(NP):
        live = jnp.where(rows < AB, sig[0, p_index[s]], sig[1, p_index[s]]) > 0
        gamma = jnp.where(live, acc[:, s * V : (s + 1) * V], 0.0)
        out[:, s] = gamma.reshape(16, 16, V)


def pairs(sig, keep, occ, virt, *blocks):
    smem = pl.BlockSpec(memory_space=pltpu.SMEM)
    vmem = pl.BlockSpec(memory_space=pltpu.VMEM)
    return pl.pallas_call(
        pair_kernel,
        out_shape=jax.ShapeDtypeStruct((16, NP, 16, V), jnp.float32),
        in_specs=[smem] * 3 + [vmem] * (1 + len(blocks)),
        out_specs=vmem,
        scratch_shapes=[
            pltpu.VMEM((NA, NP * V), jnp.bfloat16),
            pltpu.VMEM((NP * V, NA), jnp.bfloat16),
            pltpu.VMEM((NC, NA, 2 * V), jnp.bfloat16),
            pltpu.VMEM((V, V), jnp.float32),
            pltpu.VMEM((NA, NP * V), jnp.float32),
        ],
        compiler_params=pltpu.CompilerParams(vmem_limit_bytes=24 * 2**20),
        cost_estimate=pl.CostEstimate(flops=2 * 10**9, bytes_accessed=2 * 10**6, transcendentals=10**6),
    )(sig, keep, occ, virt, *blocks)


def spread(x, axis, size):
    return lax.all_to_all(jnp.broadcast_to(x, (size,) + x.shape), axis, 0, 0, tiled=True)


def ahead(x, shift):
    pairs = [(i, (i - shift) % NZ) for i in range(NZ)]
    return lax.ppermute(x, ("blk_far", "blk_near"), pairs)


def on_device(b_tensor, significance, pair_keep, occ_energy, virt_energy):
    own = lax.all_to_all(b_tensor[0], AUX, 0, 0, tiled=True).reshape(NA, V)
    q0 = spread(own, "blk_far", NH)
    p_blocks = spread(own, "blk_y", NP)
    q1, q3 = ahead(q0, 1), ahead(q0, -1)
    q2a, q2b = ahead(q0[:2], 2), ahead(q0[2:], -2)
    part = pairs(
        significance[:, 0, :].T, pair_keep[0], occ_energy.T, virt_energy, p_blocks, q0, q1, q2a, q2b, q3
    )
    back = lax.all_to_all(part.reshape(64, 16, V), AUX + ("blk_y",), 0, 0, tiled=True)
    return back.reshape(16, NP, 16, V).sum(axis=1)[None]


def solution(mesh):
    blk = ("blk_y", "blk_far", "blk_near")
    fine = Mesh(mesh.devices.reshape(4, 2, 2, NP, NH, NL), AUX + blk)
    return jax.shard_map(
        on_device,
        mesh=fine,
        in_specs=(
            P(blk, None, AUX, None),
            P(None, AUX, None),
            P(AUX, None, None),
            P(None, AUX),
            P(AUX, None),
        ),
        out_specs=P(blk, None, AUX, None),
        check_vma=False,
    )
```

```python
import functools

import jax
import jax.numpy as jnp
from jax import lax
from jax.experimental import pallas as pl
from jax.experimental.pallas import tpu as pltpu
from jax.sharding import Mesh, PartitionSpec as P

AUX = ("aux_x", "aux_y", "aux_core")
NP = 4
NZ = 16
EARLY = (5, -5, 1, 6, -4, -1, 4, -6)
LATE = (0, 2, 7, -3, -2, 3, -7, 8)
V = 128
AB = 128
NA = 256


def pair_kernel(shifts, finish, sig, keep, occ, virt, p_ref, *refs):
    counts = [ref.shape[0] for ref in refs if len(ref.shape) == 3 and ref.shape[1:] == (NA, V)]
    q_refs, refs = refs[: len(counts)], refs[len(counts) :]
    if finish:
        before, out, pcat, pcat_t, vb, acc = refs
    else:
        acc, pcat, pcat_t, vb = refs
    h = lax.axis_index("blk_y")
    w = lax.axis_index("blk_z")
    rows = lax.broadcasted_iota(jnp.int32, (NA, V), 0)
    zero = jnp.zeros((NA, V), jnp.bfloat16)

    def live(orbital):
        return jnp.where(rows < AB, sig[0, orbital], sig[1, orbital]) > 0

    p_index = [s * NZ + w for s in range(NP)]
    for s in range(NP):
        block = jnp.where(live(p_index[s]), p_ref[s], zero)
        pcat[:, s * V : (s + 1) * V] = block * 2
        pcat_t[s * V : (s + 1) * V, :] = block.T
    q_blocks = [ref.at[i] for ref, n in zip(q_refs, counts) for i in range(n)]
    q_index = [h * NZ + lax.rem(w + shift + NZ, NZ) for shift in shifts]
    va = virt[...]
    vb[...] = jnp.broadcast_to(va, (V, V)).T
    for c in range(0, len(shifts), 2):
        block = jnp.concatenate(
            [jnp.where(live(q_index[c + t]), q_blocks[c + t][...], zero) for t in range(2)], axis=1
        )
        twice = jnp.dot(block.T, pcat[...], preferred_element_type=jnp.float32)
        swapped = jnp.dot(pcat_t[...], block, preferred_element_type=jnp.float32)
        columns = []
        for s in range(NP):
            tiles = []
            for t in range(2):
                p, q = p_index[s], q_index[c + t]
                kept = keep[lax.min(p, q), lax.max(p, q)].astype(jnp.float32)
                total = occ[0, p] + occ[0, q]
                top = twice[t * V : (t + 1) * V, s * V : (s + 1) * V]
                top = top - swapped[s * V : (s + 1) * V, t * V : (t + 1) * V]
                tiles.append((kept * top / ((total - va) - vb[...])).astype(jnp.bfloat16))
            columns.append(jnp.concatenate(tiles, axis=0))
        tilde = jnp.concatenate(columns, axis=1)
        gamma = jnp.dot(block, tilde, preferred_element_type=jnp.float32)
        if c == 0:
            acc[...] = before[...] + gamma if finish else gamma
        else:
            acc[...] += gamma
    if finish:
        for s in range(NP):
            gamma = jnp.where(live(p_index[s]), acc[:, s * V : (s + 1) * V], 0.0)
            out[:, s] = gamma.reshape(16, 16, V)


def pair_terms(shifts, scalars, p_blocks, q_blocks, before=None):
    smem = pl.BlockSpec(memory_space=pltpu.SMEM)
    vmem = pl.BlockSpec(memory_space=pltpu.VMEM)
    sums = (NA, NP * V)
    arrays = [p_blocks, *q_blocks] + ([] if before is None else [before])
    return pl.pallas_call(
        functools.partial(pair_kernel, shifts, before is not None),
        out_shape=jax.ShapeDtypeStruct(sums if before is None else (16, NP, 16, V), jnp.float32),
        in_specs=[smem] * 3 + [vmem] * (1 + len(arrays)),
        out_specs=vmem,
        scratch_shapes=[
            pltpu.VMEM((NA, NP * V), jnp.bfloat16),
            pltpu.VMEM((NP * V, NA), jnp.bfloat16),
            pltpu.VMEM((V, V), jnp.float32),
        ]
        + ([] if before is None else [pltpu.VMEM(sums, jnp.float32)]),
        compiler_params=pltpu.CompilerParams(vmem_limit_bytes=24 * 2**20),
        cost_estimate=pl.CostEstimate(flops=10**9, bytes_accessed=2 * 10**6, transcendentals=5 * 10**5),
    )(*scalars, *arrays)


def ahead(x, shift):
    return lax.ppermute(x, "blk_z", [(i, (i - shift) % NZ) for i in range(NZ)])


def on_device(b_tensor, significance, pair_keep, occ_energy, virt_energy):
    own = lax.all_to_all(b_tensor[0], AUX, 0, 0, tiled=True).reshape(1, NA, V)
    up, down = ahead(own, 5), ahead(own, -5)
    p_blocks = lax.all_to_all(jnp.broadcast_to(own, (NP, NA, V)), "blk_y", 0, 0, tiled=True)
    three = jnp.concatenate([own, up, down], axis=0)
    scalars = (significance[:, 0, :].T, pair_keep[0], occ_energy.T, virt_energy)
    early = [up, down, ahead(three, 1), ahead(three, -1)]
    late = [own, ahead(three, 2), ahead(three, -2), ahead(up, 3)]
    part = pair_terms(EARLY, scalars, p_blocks, early)
    part = pair_terms(LATE, scalars, p_blocks, late, part)
    back = lax.all_to_all(part.reshape(64, 16, V), AUX + ("blk_y",), 0, 0, tiled=True)
    return back.reshape(16, NP, 16, V).sum(axis=1)[None]


def solution(mesh):
    fine = Mesh(mesh.devices.reshape(4, 2, 2, NP, NZ), AUX + ("blk_y", "blk_z"))
    blk = ("blk_y", "blk_z")
    return jax.shard_map(
        on_device,
        mesh=fine,
        in_specs=(
            P(blk, None, AUX, None),
            P(None, AUX, None),
            P(AUX, None, None),
            P(None, AUX),
            P(AUX, None),
        ),
        out_specs=P(blk, None, AUX, None),
        check_vma=False,
    )
```

```python
import functools

import jax
import jax.numpy as jnp
from jax import lax
from jax.experimental import pallas as pl
from jax.experimental.pallas import tpu as pltpu
from jax.sharding import Mesh, PartitionSpec as P

AUX = ("aux_x", "aux_y", "aux_core")
NP = 4
NZ = 16
NF = NZ // 2
V = 128
AB = 128
NA = 256


def pair_kernel(parity, finish, sig, keep, occ, virt, p_ref, *refs):
    counts = [ref.shape[0] for ref in refs if len(ref.shape) == 3 and ref.shape[1:] == (NA, V)]
    q_refs, refs = refs[: len(counts)], refs[len(counts) :]
    if finish:
        before, out, pcat, pcat_t, vb, acc = refs
    else:
        acc, pcat, pcat_t, vb = refs
    h = lax.axis_index("blk_y")
    near = lax.axis_index("blk_near")
    w = 2 * lax.axis_index("blk_far") + near
    rows = lax.broadcasted_iota(jnp.int32, (NA, V), 0)
    zero = jnp.zeros((NA, V), jnp.bfloat16)

    def live(orbital):
        return jnp.where(rows < AB, sig[0, orbital], sig[1, orbital]) > 0

    p_index = [s * NZ + w for s in range(NP)]
    for s in range(NP):
        block = jnp.where(live(p_index[s]), p_ref[s], zero)
        pcat[:, s * V : (s + 1) * V] = block * 2
        pcat_t[s * V : (s + 1) * V, :] = block.T
    q_blocks = [ref.at[i] for ref, n in zip(q_refs, counts) for i in range(n)]
    near = near if parity == 0 else 1 - near
    q_index = [h * NZ + 2 * far + near for far in range(NF)]
    va = virt[...]
    vb[...] = jnp.broadcast_to(va, (V, V)).T
    for c in range(0, NF, 2):
        block = jnp.concatenate(
            [jnp.where(live(q_index[c + t]), q_blocks[c + t][...], zero) for t in range(2)], axis=1
        )
        twice = jnp.dot(block.T, pcat[...], preferred_element_type=jnp.float32)
        swapped = jnp.dot(pcat_t[...], block, preferred_element_type=jnp.float32)
        columns = []
        for s in range(NP):
            tiles = []
            for t in range(2):
                p, q = p_index[s], q_index[c + t]
                kept = keep[lax.min(p, q), lax.max(p, q)].astype(jnp.float32)
                total = occ[0, p] + occ[0, q]
                top = twice[t * V : (t + 1) * V, s * V : (s + 1) * V]
                top = top - swapped[s * V : (s + 1) * V, t * V : (t + 1) * V]
                tiles.append((kept * top / ((total - va) - vb[...])).astype(jnp.bfloat16))
            columns.append(jnp.concatenate(tiles, axis=0))
        tilde = jnp.concatenate(columns, axis=1)
        gamma = jnp.dot(block, tilde, preferred_element_type=jnp.float32)
        if c == 0:
            acc[...] = before[...] + gamma if finish else gamma
        else:
            acc[...] += gamma
    if finish:
        for s in range(NP):
            gamma = jnp.where(live(p_index[s]), acc[:, s * V : (s + 1) * V], 0.0)
            out[:, s] = gamma.reshape(16, 16, V)


def pair_terms(parity, scalars, p_blocks, q_blocks, before=None):
    smem = pl.BlockSpec(memory_space=pltpu.SMEM)
    vmem = pl.BlockSpec(memory_space=pltpu.VMEM)
    sums = (NA, NP * V)
    arrays = [p_blocks, *q_blocks] + ([] if before is None else [before])
    return pl.pallas_call(
        functools.partial(pair_kernel, parity, before is not None),
        out_shape=jax.ShapeDtypeStruct(sums if before is None else (16, NP, 16, V), jnp.float32),
        in_specs=[smem] * 3 + [vmem] * (1 + len(arrays)),
        out_specs=vmem,
        scratch_shapes=[
            pltpu.VMEM((NA, NP * V), jnp.bfloat16),
            pltpu.VMEM((NP * V, NA), jnp.bfloat16),
            pltpu.VMEM((V, V), jnp.float32),
        ]
        + ([] if before is None else [pltpu.VMEM(sums, jnp.float32)]),
        compiler_params=pltpu.CompilerParams(vmem_limit_bytes=24 * 2**20),
        cost_estimate=pl.CostEstimate(flops=10**9, bytes_accessed=2 * 10**6, transcendentals=5 * 10**5),
    )(*scalars, *arrays)


def ahead(x, shift):
    return lax.ppermute(x, ("blk_far", "blk_near"), [(i, (i - shift) % NZ) for i in range(NZ)])


def on_device(b_tensor, significance, pair_keep, occ_energy, virt_energy):
    own = lax.all_to_all(b_tensor[0], AUX, 0, 0, tiled=True).reshape(1, NA, V)
    p_blocks = lax.all_to_all(jnp.broadcast_to(own, (NP, NA, V)), "blk_y", 0, 0, tiled=True)
    same = lax.all_gather(own, "blk_far", axis=0, tiled=True)
    other = [ahead(same[: NF // 2], 1), ahead(same[NF // 2 :], -1)]
    scalars = (significance[:, 0, :].T, pair_keep[0], occ_energy.T, virt_energy)
    part = pair_terms(0, scalars, p_blocks, [same])
    part = pair_terms(1, scalars, p_blocks, other, part)
    back = lax.all_to_all(part.reshape(64, 16, V), AUX + ("blk_y",), 0, 0, tiled=True)
    return back.reshape(16, NP, 16, V).sum(axis=1)[None]


def solution(mesh):
    blk = ("blk_y", "blk_far", "blk_near")
    fine = Mesh(mesh.devices.reshape(4, 2, 2, NP, NF, 2), AUX + blk)
    return jax.shard_map(
        on_device,
        mesh=fine,
        in_specs=(
            P(blk, None, AUX, None),
            P(None, AUX, None),
            P(AUX, None, None),
            P(None, AUX),
            P(AUX, None),
        ),
        out_specs=P(blk, None, AUX, None),
        check_vma=False,
    )
```

```python
import functools

import jax
import jax.numpy as jnp
from jax import lax
from jax.experimental import pallas as pl
from jax.experimental.pallas import tpu as pltpu
from jax.sharding import Mesh, PartitionSpec as P

AUX = ("aux_x", "aux_y", "aux_core")
NP = 4
NZ = 16
NF = NZ // 2
V = 128
AB = 128
NA = 256


def pair_kernel(parity, finish, sig, keep, occ, virt, p_ref, *refs):
    counts = [ref.shape[0] for ref in refs if len(ref.shape) == 3 and ref.shape[1:] == (NA, V)]
    q_refs, refs = refs[: len(counts)], refs[len(counts) :]
    if finish:
        before, out, pcat, pcat_t, vb, acc = refs
    else:
        acc, pcat, pcat_t, vb = refs
    h = lax.axis_index("blk_y")
    near = lax.axis_index("blk_near")
    w = 2 * lax.axis_index("blk_far") + near
    rows = lax.broadcasted_iota(jnp.int32, (NA, V), 0)
    zero = jnp.zeros((NA, V), jnp.bfloat16)

    def live(orbital):
        return jnp.where(rows < AB, sig[0, orbital], sig[1, orbital]) > 0

    p_index = [s * NZ + w for s in range(NP)]
    for s in range(NP):
        block = jnp.where(live(p_index[s]), p_ref[s], zero)
        pcat[:, s * V : (s + 1) * V] = block * 2
        pcat_t[s * V : (s + 1) * V, :] = block.T
    q_blocks = [ref.at[i] for ref, n in zip(q_refs, counts) for i in range(n)]
    near = near if parity == 0 else 1 - near
    q_index = [h * NZ + 2 * far + near for far in range(NF)]
    va = virt[...]
    vb[...] = jnp.broadcast_to(va, (V, V)).T
    for c in range(0, NF, 2):
        block = jnp.concatenate(
            [jnp.where(live(q_index[c + t]), q_blocks[c + t][...], zero) for t in range(2)], axis=1
        )
        twice = jnp.dot(block.T, pcat[...], preferred_element_type=jnp.float32)
        swapped = jnp.dot(pcat_t[...], block, preferred_element_type=jnp.float32)
        columns = []
        for s in range(NP):
            tiles = []
            for t in range(2):
                p, q = p_index[s], q_index[c + t]
                kept = keep[lax.min(p, q), lax.max(p, q)].astype(jnp.float32)
                total = occ[0, p] + occ[0, q]
                top = twice[t * V : (t + 1) * V, s * V : (s + 1) * V]
                top = top - swapped[s * V : (s + 1) * V, t * V : (t + 1) * V]
                tiles.append((kept * top / ((total - va) - vb[...])).astype(jnp.bfloat16))
            columns.append(jnp.concatenate(tiles, axis=0))
        tilde = jnp.concatenate(columns, axis=1)
        gamma = jnp.dot(block, tilde, preferred_element_type=jnp.float32)
        if c == 0:
            acc[...] = before[...] + gamma if finish else gamma
        else:
            acc[...] += gamma
    if finish:
        for s in range(NP):
            gamma = jnp.where(live(p_index[s]), acc[:, s * V : (s + 1) * V], 0.0)
            out[s] = gamma.reshape(16, 16, V)


def pair_terms(parity, scalars, p_blocks, q_blocks, before=None):
    smem = pl.BlockSpec(memory_space=pltpu.SMEM)
    vmem = pl.BlockSpec(memory_space=pltpu.VMEM)
    sums = (NA, NP * V)
    arrays = [p_blocks, *q_blocks] + ([] if before is None else [before])
    return pl.pallas_call(
        functools.partial(pair_kernel, parity, before is not None),
        out_shape=jax.ShapeDtypeStruct(sums if before is None else (NP, 16, 16, V), jnp.float32),
        in_specs=[smem] * 3 + [vmem] * (1 + len(arrays)),
        out_specs=vmem,
        scratch_shapes=[
            pltpu.VMEM((NA, NP * V), jnp.bfloat16),
            pltpu.VMEM((NP * V, NA), jnp.bfloat16),
            pltpu.VMEM((V, V), jnp.float32),
        ]
        + ([] if before is None else [pltpu.VMEM(sums, jnp.float32)]),
        compiler_params=pltpu.CompilerParams(vmem_limit_bytes=24 * 2**20),
        cost_estimate=pl.CostEstimate(flops=10**9, bytes_accessed=2 * 10**6, transcendentals=5 * 10**5),
    )(*scalars, *arrays)


def ahead(x, shift):
    return lax.ppermute(x, ("blk_far", "blk_near"), [(i, (i - shift) % NZ) for i in range(NZ)])


def on_device(b_tensor, significance, pair_keep, occ_energy, virt_energy):
    own = lax.all_to_all(b_tensor[0], AUX, 0, 0, tiled=True).reshape(1, NA, V)
    same = lax.all_gather(own, "blk_far", axis=0, tiled=True)
    own, same = lax.optimization_barrier((own, same))
    p_blocks = lax.all_to_all(jnp.broadcast_to(own, (NP, NA, V)), "blk_y", 0, 0, tiled=True)
    other = [ahead(same[: NF // 2], 1), ahead(same[NF // 2 :], -1)]
    scalars = (significance[:, 0, :].T, pair_keep[0], occ_energy.T, virt_energy)
    part = pair_terms(0, scalars, p_blocks, [same])
    part = pair_terms(1, scalars, p_blocks, other, part)
    back = lax.all_to_all(part.reshape(64, 16, V), ("blk_y",) + AUX, 0, 0, tiled=True)
    return back.reshape(NP, 16, 16, V).sum(axis=0)[None]


def solution(mesh):
    blk = ("blk_y", "blk_far", "blk_near")
    fine = Mesh(mesh.devices.reshape(4, 2, 2, NP, NF, 2), AUX + blk)
    return jax.shard_map(
        on_device,
        mesh=fine,
        in_specs=(
            P(blk, None, AUX, None),
            P(None, AUX, None),
            P(AUX, None, None),
            P(None, AUX),
            P(AUX, None),
        ),
        out_specs=P(blk, None, AUX, None),
        check_vma=False,
    )
```

```python
import jax
import jax.numpy as jnp
from jax import lax
from jax.experimental import pallas as pl
from jax.experimental.pallas import tpu as pltpu
from jax.sharding import Mesh, PartitionSpec as P

AUX = ("aux_x", "aux_y", "aux_core")
NP = 4
NZ = 16
SCALE = 2.0**14
V = 128
AB = 128
NA = 256


def pair_kernel(sig, keep, occ, virt, p_ref, q_ref, out, pcat, pcat_t, vb, acc):
    h = lax.axis_index("blk_y")
    w = lax.axis_index("blk_z")
    rows = lax.broadcasted_iota(jnp.int32, (NA, V), 0)
    zero = jnp.zeros((NA, V), jnp.bfloat16)

    def live(orbital):
        return jnp.where(rows < AB, sig[0, orbital], sig[1, orbital]) > 0

    p_index = [s * NZ + w for s in range(NP)]
    for s in range(NP):
        block = jnp.where(live(p_index[s]), p_ref[s], zero) * (1 / SCALE)
        pcat[:, s * V : (s + 1) * V] = block * 2
        pcat_t[s * V : (s + 1) * V, :] = block.T
    q_index = [h * NZ + k for k in range(NZ)]
    va = virt[...]
    vb[...] = jnp.broadcast_to(va, (V, V)).T
    for c in range(0, NZ, 2):
        block = jnp.concatenate([jnp.where(live(q_index[c + t]), q_ref[c + t], zero) for t in range(2)], axis=1)
        twice = jnp.dot(block.T, pcat[...], preferred_element_type=jnp.float32)
        swapped = jnp.dot(pcat_t[...], block, preferred_element_type=jnp.float32)
        columns = []
        for s in range(NP):
            tiles = []
            for t in range(2):
                p, q = p_index[s], q_index[c + t]
                kept = keep[lax.min(p, q), lax.max(p, q)].astype(jnp.float32)
                total = occ[0, p] + occ[0, q]
                top = twice[t * V : (t + 1) * V, s * V : (s + 1) * V]
                top = top - swapped[s * V : (s + 1) * V, t * V : (t + 1) * V]
                tiles.append((kept * top / ((total - va) - vb[...])).astype(jnp.bfloat16))
            columns.append(jnp.concatenate(tiles, axis=0))
        tilde = jnp.concatenate(columns, axis=1)
        gamma = jnp.dot(block, tilde, preferred_element_type=jnp.float32)
        if c == 0:
            acc[...] = gamma
        else:
            acc[...] += gamma
    for s in range(NP):
        gamma = jnp.where(live(p_index[s]), acc[:, s * V : (s + 1) * V], 0.0) * (1 / SCALE)
        out[s] = gamma.reshape(16, 16, V)


def pair_terms(scalars, p_blocks, q_blocks):
    smem = pl.BlockSpec(memory_space=pltpu.SMEM)
    vmem = pl.BlockSpec(memory_space=pltpu.VMEM)
    return pl.pallas_call(
        pair_kernel,
        out_shape=jax.ShapeDtypeStruct((NP, 16, 16, V), jnp.float32),
        in_specs=[smem] * 3 + [vmem] * 3,
        out_specs=vmem,
        scratch_shapes=[
            pltpu.VMEM((NA, NP * V), jnp.bfloat16),
            pltpu.VMEM((NP * V, NA), jnp.bfloat16),
            pltpu.VMEM((V, V), jnp.float32),
            pltpu.VMEM((NA, NP * V), jnp.float32),
        ],
        compiler_params=pltpu.CompilerParams(vmem_limit_bytes=24 * 2**20),
        cost_estimate=pl.CostEstimate(flops=2 * 10**9, bytes_accessed=2 * 10**6, transcendentals=10**6),
    )(*scalars, p_blocks, q_blocks)


def on_device(b_tensor, significance, pair_keep, occ_energy, virt_energy):
    own = lax.all_to_all(b_tensor[0], AUX, 0, 0, tiled=True).reshape(1, NA, V)
    sent = (own.astype(jnp.float32) * SCALE).astype(jnp.float16)
    line = lax.all_gather(sent, "blk_z", axis=0, tiled=True)
    own, line = lax.optimization_barrier((own, line))
    p_blocks = lax.all_to_all(jnp.broadcast_to(own, (NP, NA, V)), "blk_y", 0, 0, tiled=True)
    scalars = (significance[:, 0, :].T, pair_keep[0], occ_energy.T, virt_energy)
    part = pair_terms(scalars, p_blocks, line.astype(jnp.bfloat16))
    back = lax.all_to_all(part.reshape(64, 16, V), ("blk_y",) + AUX, 0, 0, tiled=True)
    return back.reshape(NP, 16, 16, V).sum(axis=0)[None]


def solution(mesh):
    blk = ("blk_y", "blk_z")
    fine = Mesh(mesh.devices.reshape(4, 2, 2, NP, NZ), AUX + blk)
    return jax.shard_map(
        on_device,
        mesh=fine,
        in_specs=(
            P(blk, None, AUX, None),
            P(None, AUX, None),
            P(AUX, None, None),
            P(None, AUX),
            P(AUX, None),
        ),
        out_specs=P(blk, None, AUX, None),
        check_vma=False,
    )
```

```python
import jax
import jax.numpy as jnp
from jax import lax
from jax.experimental import pallas as pl
from jax.experimental.pallas import tpu as pltpu
from jax.sharding import Mesh, PartitionSpec as P

AUX = ("aux_x", "aux_y", "aux_core")
NP = 4
NZ = 16
SCALE = 2.0**14
V = 128
AB = 128
NA = 256


def pair_kernel(sig, keep, occ, virt, p_ref, q_ref, out, pcat, pcat_t, vb, acc):
    h = lax.axis_index("blk_y")
    w = lax.axis_index("blk_z")
    rows = lax.broadcasted_iota(jnp.int32, (NA, V), 0)
    zero = jnp.zeros((NA, V), jnp.bfloat16)

    def live(orbital):
        return jnp.where(rows < AB, sig[0, orbital], sig[1, orbital]) > 0

    p_index = [s * NZ + w for s in range(NP)]
    for s in range(NP):
        block = jnp.where(live(p_index[s]), p_ref[s], zero) * (1 / SCALE)
        pcat[:, s * V : (s + 1) * V] = block * 2
        pcat_t[s * V : (s + 1) * V, :] = block.T
    q_index = [h * NZ + k for k in range(NZ)]
    va = virt[...]
    vb[...] = jnp.broadcast_to(va, (V, V)).T
    for c in range(0, NZ, 2):
        block = jnp.concatenate([jnp.where(live(q_index[c + t]), q_ref[c + t], zero) for t in range(2)], axis=1)
        twice = jnp.dot(block.T, pcat[...], preferred_element_type=jnp.float32)
        swapped = jnp.dot(pcat_t[...], block, preferred_element_type=jnp.float32)
        columns = []
        for s in range(NP):
            tiles = []
            for t in range(2):
                p, q = p_index[s], q_index[c + t]
                kept = keep[lax.min(p, q), lax.max(p, q)].astype(jnp.float32)
                total = occ[0, p] + occ[0, q]
                top = twice[t * V : (t + 1) * V, s * V : (s + 1) * V]
                top = top - swapped[s * V : (s + 1) * V, t * V : (t + 1) * V]
                tiles.append((kept * top / ((total - va) - vb[...])).astype(jnp.bfloat16))
            columns.append(jnp.concatenate(tiles, axis=0))
        tilde = jnp.concatenate(columns, axis=1)
        gamma = jnp.dot(block, tilde, preferred_element_type=jnp.float32)
        if c == 0:
            acc[...] = gamma
        else:
            acc[...] += gamma
    for s in range(NP):
        gamma = jnp.where(live(p_index[s]), acc[:, s * V : (s + 1) * V], 0.0) * (1 / SCALE)
        out[s] = gamma.reshape(16, 16, V)


def pair_terms(scalars, p_blocks, q_blocks):
    smem = pl.BlockSpec(memory_space=pltpu.SMEM)
    vmem = pl.BlockSpec(memory_space=pltpu.VMEM)
    return pl.pallas_call(
        pair_kernel,
        out_shape=jax.ShapeDtypeStruct((NP, 16, 16, V), jnp.float32),
        in_specs=[smem] * 3 + [vmem] * 3,
        out_specs=vmem,
        scratch_shapes=[
            pltpu.VMEM((NA, NP * V), jnp.bfloat16),
            pltpu.VMEM((NP * V, NA), jnp.bfloat16),
            pltpu.VMEM((V, V), jnp.float32),
            pltpu.VMEM((NA, NP * V), jnp.float32),
        ],
        compiler_params=pltpu.CompilerParams(vmem_limit_bytes=24 * 2**20),
        cost_estimate=pl.CostEstimate(flops=2 * 10**9, bytes_accessed=2 * 10**6, transcendentals=10**6),
    )(*scalars, p_blocks, q_blocks)


def on_device(b_tensor, significance, pair_keep, occ_energy, virt_energy):
    own = lax.all_to_all(b_tensor[0], AUX, 0, 0, tiled=True).reshape(1, NA, V)
    p_blocks = lax.all_to_all(jnp.broadcast_to(own, (NP, NA, V)), "blk_y", 0, 0, tiled=True)
    sent = (own.astype(jnp.float32) * SCALE).astype(jnp.float16)
    line = lax.all_gather(sent, "blk_z", axis=0, tiled=True)
    scalars = (significance[:, 0, :].T, pair_keep[0], occ_energy.T, virt_energy)
    part = pair_terms(scalars, p_blocks, line.astype(jnp.bfloat16))
    back = lax.all_to_all(part.reshape(64, 16, V), ("blk_y",) + AUX, 0, 0, tiled=True)
    return back.reshape(NP, 16, 16, V).sum(axis=0)[None]


def solution(mesh):
    blk = ("blk_y", "blk_z")
    fine = Mesh(mesh.devices.reshape(4, 2, 2, NP, NZ), AUX + blk)
    return jax.shard_map(
        on_device,
        mesh=fine,
        in_specs=(
            P(blk, None, AUX, None),
            P(None, AUX, None),
            P(AUX, None, None),
            P(None, AUX),
            P(AUX, None),
        ),
        out_specs=P(blk, None, AUX, None),
        check_vma=False,
    )
```

```python
import jax
import jax.numpy as jnp
from jax import lax
from jax.experimental import pallas as pl
from jax.experimental.pallas import tpu as pltpu
from jax.sharding import Mesh, PartitionSpec as P

AUX = ("aux_x", "aux_y", "aux_core")
NP = 4
NZ = 16
SCALE = 2.0**14
V = 128
AB = 128
NA = 256


def pair_kernel(sig_hbm, keep_hbm, occ_hbm, virt, p_ref, q_ref, out, pcat, pcat_t, vb, sig, keep, occ, done):
    copies = [
        pltpu.make_async_copy(src, dst, done.at[i])
        for i, (src, dst) in enumerate(((sig_hbm, sig), (keep_hbm, keep), (occ_hbm, occ)))
    ]
    for copy in copies:
        copy.start()
    va = virt[...]
    vb[...] = jnp.broadcast_to(va, (V, V)).T
    for copy in copies:
        copy.wait()
    h = lax.axis_index("blk_y")
    w = lax.axis_index("blk_z")
    rows = lax.broadcasted_iota(jnp.int32, (NA, V), 0)
    zero = jnp.zeros((NA, V), jnp.bfloat16)

    def live(orbital):
        return jnp.where(rows < AB, sig[0, orbital], sig[1, orbital]) > 0

    p_index = [s * NZ + w for s in range(NP)]
    for s in range(NP):
        block = jnp.where(live(p_index[s]), p_ref[s], zero) * (1 / SCALE)
        pcat[:, s * V : (s + 1) * V] = block * 2
        pcat_t[s * V : (s + 1) * V, :] = block.T
    q_index = [h * NZ + k for k in range(NZ)]
    qs, ts = [], []
    for c in range(0, NZ, 2):
        block = jnp.concatenate([jnp.where(live(q_index[c + t]), q_ref[c + t], zero) for t in range(2)], axis=1)
        twice = jnp.dot(block.T, pcat[...], preferred_element_type=jnp.float32)
        swapped = jnp.dot(pcat_t[...], block, preferred_element_type=jnp.float32)
        columns = []
        for s in range(NP):
            tiles = []
            for t in range(2):
                p, q = p_index[s], q_index[c + t]
                kept = keep[lax.min(p, q), lax.max(p, q)].astype(jnp.float32)
                total = occ[0, p] + occ[0, q]
                top = twice[t * V : (t + 1) * V, s * V : (s + 1) * V]
                top = top - swapped[s * V : (s + 1) * V, t * V : (t + 1) * V]
                tiles.append((kept * top / ((total - va) - vb[...])).astype(jnp.bfloat16))
            columns.append(jnp.concatenate(tiles, axis=0))
        tilde = jnp.concatenate(columns, axis=1)
        qs.append(block)
        ts.append(tilde)
    gammas = jnp.dot(jnp.concatenate(qs, axis=1), jnp.concatenate(ts, axis=0), preferred_element_type=jnp.float32)
    for s in range(NP):
        gamma = jnp.where(live(p_index[s]), gammas[:, s * V : (s + 1) * V], 0.0) * (1 / SCALE)
        out[s] = gamma.reshape(16, 16, V)


def pair_terms(scalars, p_blocks, q_blocks):
    hbm = pl.BlockSpec(memory_space=pltpu.HBM)
    vmem = pl.BlockSpec(memory_space=pltpu.VMEM)
    return pl.pallas_call(
        pair_kernel,
        out_shape=jax.ShapeDtypeStruct((NP, 16, 16, V), jnp.float32),
        in_specs=[hbm] * 3 + [vmem] * 3,
        out_specs=vmem,
        scratch_shapes=[
            pltpu.VMEM((NA, NP * V), jnp.bfloat16),
            pltpu.VMEM((NP * V, NA), jnp.bfloat16),
            pltpu.VMEM((V, V), jnp.float32),
            pltpu.SMEM((2, NP * NZ), jnp.int32),
            pltpu.SMEM((NP * NZ, NP * NZ), jnp.int32),
            pltpu.SMEM((1, NP * NZ), jnp.float32),
            pltpu.SemaphoreType.DMA((3,)),
        ],
        compiler_params=pltpu.CompilerParams(vmem_limit_bytes=24 * 2**20),
        cost_estimate=pl.CostEstimate(flops=2 * 10**9, bytes_accessed=2 * 10**6, transcendentals=10**6),
    )(*scalars, p_blocks, q_blocks)


def on_device(b_tensor, significance, pair_keep, occ_energy, virt_energy):
    own = lax.all_to_all(b_tensor[0], AUX, 0, 0, tiled=True).reshape(1, NA, V)
    p_blocks = lax.all_to_all(jnp.broadcast_to(own, (NP, NA, V)), "blk_y", 0, 0, tiled=True)
    sent = (own.astype(jnp.float32) * SCALE).astype(jnp.float16)
    line = lax.all_gather(sent, "blk_z", axis=0, tiled=True)
    scalars = (significance[:, 0, :].T, pair_keep[0], occ_energy.T, virt_energy)
    part = pair_terms(scalars, p_blocks, line.astype(jnp.bfloat16))
    back = lax.all_to_all(part.reshape(64, 16, V), ("blk_y",) + AUX, 0, 0, tiled=True)
    return back.reshape(NP, 16, 16, V).sum(axis=0)[None]


def solution(mesh):
    blk = ("blk_y", "blk_z")
    fine = Mesh(mesh.devices.reshape(4, 2, 2, NP, NZ), AUX + blk)
    return jax.shard_map(
        on_device,
        mesh=fine,
        in_specs=(
            P(blk, None, AUX, None),
            P(None, AUX, None),
            P(AUX, None, None),
            P(None, AUX),
            P(AUX, None),
        ),
        out_specs=P(blk, None, AUX, None),
        check_vma=False,
    )
```

```python
import jax
import jax.numpy as jnp
from jax import lax
from jax.experimental import pallas as pl
from jax.experimental.pallas import tpu as pltpu
from jax.sharding import Mesh, PartitionSpec as P

AUX = ("aux_x", "aux_y", "aux_core")
NP = 4
NZ = 16
RINGS = [list(range(NZ)), list(range(2 * NZ - 1, NZ - 1, -1))]
SCALE = 2.0**14
V = 128
AB = 128
NA = 256


def pair_kernel(sig_hbm, keep_hbm, occ_hbm, virt, p_ref, q_ref, out, pcat, pcat_t, vb, sig, keep, occ, done):
    copies = [
        pltpu.make_async_copy(src, dst, done.at[i])
        for i, (src, dst) in enumerate(((sig_hbm, sig), (keep_hbm, keep), (occ_hbm, occ)))
    ]
    for copy in copies:
        copy.start()
    va = virt[...]
    vb[...] = jnp.broadcast_to(va, (V, V)).T
    for copy in copies:
        copy.wait()
    h = lax.axis_index("blk_y")
    w = lax.axis_index("blk_z")
    rows = lax.broadcasted_iota(jnp.int32, (NA, V), 0)
    zero = jnp.zeros((NA, V), jnp.bfloat16)

    def live(orbital):
        return jnp.where(rows < AB, sig[0, orbital], sig[1, orbital]) > 0

    p_index = [s * NZ + w for s in range(NP)]
    for s in range(NP):
        block = jnp.where(live(p_index[s]), p_ref[s], zero) * (1 / SCALE)
        pcat[:, s * V : (s + 1) * V] = block * 2
        pcat_t[s * V : (s + 1) * V, :] = block.T
    core = lax.axis_index("aux_core")
    q_index = [h * NZ + jnp.where(core == 0, k, NZ - 1 - k) for k in range(NZ)]
    qs, ts = [], []
    for c in range(0, NZ, 2):
        block = jnp.concatenate([jnp.where(live(q_index[c + t]), q_ref[c + t], zero) for t in range(2)], axis=1)
        twice = jnp.dot(block.T, pcat[...], preferred_element_type=jnp.float32)
        swapped = jnp.dot(pcat_t[...], block, preferred_element_type=jnp.float32)
        columns = []
        for s in range(NP):
            tiles = []
            for t in range(2):
                p, q = p_index[s], q_index[c + t]
                kept = keep[lax.min(p, q), lax.max(p, q)].astype(jnp.float32)
                total = occ[0, p] + occ[0, q]
                top = twice[t * V : (t + 1) * V, s * V : (s + 1) * V]
                top = top - swapped[s * V : (s + 1) * V, t * V : (t + 1) * V]
                tiles.append((kept * top / ((total - va) - vb[...])).astype(jnp.bfloat16))
            columns.append(jnp.concatenate(tiles, axis=0))
        tilde = jnp.concatenate(columns, axis=1)
        qs.append(block)
        ts.append(tilde)
    gammas = jnp.dot(jnp.concatenate(qs, axis=1), jnp.concatenate(ts, axis=0), preferred_element_type=jnp.float32)
    for s in range(NP):
        gamma = jnp.where(live(p_index[s]), gammas[:, s * V : (s + 1) * V], 0.0) * (1 / SCALE)
        out[s] = gamma.reshape(16, 16, V)


def pair_terms(scalars, p_blocks, q_blocks):
    hbm = pl.BlockSpec(memory_space=pltpu.HBM)
    vmem = pl.BlockSpec(memory_space=pltpu.VMEM)
    return pl.pallas_call(
        pair_kernel,
        out_shape=jax.ShapeDtypeStruct((NP, 16, 16, V), jnp.float32),
        in_specs=[hbm] * 3 + [vmem] * 3,
        out_specs=vmem,
        scratch_shapes=[
            pltpu.VMEM((NA, NP * V), jnp.bfloat16),
            pltpu.VMEM((NP * V, NA), jnp.bfloat16),
            pltpu.VMEM((V, V), jnp.float32),
            pltpu.SMEM((2, NP * NZ), jnp.int32),
            pltpu.SMEM((NP * NZ, NP * NZ), jnp.int32),
            pltpu.SMEM((1, NP * NZ), jnp.float32),
            pltpu.SemaphoreType.DMA((3,)),
        ],
        compiler_params=pltpu.CompilerParams(vmem_limit_bytes=24 * 2**20),
        cost_estimate=pl.CostEstimate(flops=2 * 10**9, bytes_accessed=2 * 10**6, transcendentals=10**6),
    )(*scalars, p_blocks, q_blocks)


def on_device(b_tensor, significance, pair_keep, occ_energy, virt_energy):
    own = lax.all_to_all(b_tensor[0], AUX, 0, 0, tiled=True).reshape(1, NA, V)
    p_blocks = lax.all_to_all(jnp.broadcast_to(own, (NP, NA, V)), "blk_y", 0, 0, tiled=True)
    sent = (own.astype(jnp.float32) * SCALE).astype(jnp.float16)
    line = lax.all_gather(sent, ("aux_core", "blk_z"), axis=0, tiled=True, axis_index_groups=RINGS)
    scalars = (significance[:, 0, :].T, pair_keep[0], occ_energy.T, virt_energy)
    part = pair_terms(scalars, p_blocks, line.astype(jnp.bfloat16))
    back = lax.all_to_all(part.reshape(64, 16, V), ("blk_y",) + AUX, 0, 0, tiled=True)
    return back.reshape(NP, 16, 16, V).sum(axis=0)[None]


def solution(mesh):
    blk = ("blk_y", "blk_z")
    fine = Mesh(mesh.devices.reshape(4, 2, 2, NP, NZ), AUX + blk)
    return jax.shard_map(
        on_device,
        mesh=fine,
        in_specs=(
            P(blk, None, AUX, None),
            P(None, AUX, None),
            P(AUX, None, None),
            P(None, AUX),
            P(AUX, None),
        ),
        out_specs=P(blk, None, AUX, None),
        check_vma=False,
    )
```

```python
import jax
import jax.numpy as jnp
from jax import lax
from jax.experimental import pallas as pl
from jax.experimental.pallas import tpu as pltpu
from jax.sharding import Mesh, PartitionSpec as P

AUX = ("aux_x", "aux_y", "aux_core")
NP = 4
NZ = 16
SCALE = 2.0**14
V = 128
AB = 128
NA = 256


def pair_kernel(sig_hbm, keep_hbm, occ_hbm, virt, p_ref, q_ref, out, pcat, pcat_t, vb, sig, keep, occ, done):
    copies = [
        pltpu.make_async_copy(src, dst, done.at[i])
        for i, (src, dst) in enumerate(((sig_hbm, sig), (keep_hbm, keep), (occ_hbm, occ)))
    ]
    for copy in copies:
        copy.start()
    va = virt[...]
    vb[...] = jnp.broadcast_to(va, (V, V)).T
    for copy in copies:
        copy.wait()
    h = lax.axis_index("blk_y")
    w = lax.axis_index("blk_z")
    rows = lax.broadcasted_iota(jnp.int32, (NA, V), 0)
    zero = jnp.zeros((NA, V), jnp.bfloat16)

    def live(orbital):
        return jnp.where(rows < AB, sig[0, orbital], sig[1, orbital]) > 0

    p_index = [s * NZ + w for s in range(NP)]
    for s in range(NP):
        block = jnp.where(live(p_index[s]), p_ref[s], zero) * (1 / SCALE)
        pcat[:, s * V : (s + 1) * V] = block * 2
        pcat_t[s * V : (s + 1) * V, :] = block.T
    q_index = [h * NZ + k for k in range(NZ)]
    qs, ts = [], []
    for c in range(0, NZ, 2):
        block = jnp.concatenate([jnp.where(live(q_index[c + t]), q_ref[c + t], zero) for t in range(2)], axis=1)
        twice = jnp.dot(block.T, pcat[...], preferred_element_type=jnp.float32)
        swapped = jnp.dot(pcat_t[...], block, preferred_element_type=jnp.float32)
        columns = []
        for s in range(NP):
            tiles = []
            for t in range(2):
                p, q = p_index[s], q_index[c + t]
                kept = keep[lax.min(p, q), lax.max(p, q)].astype(jnp.float32)
                total = occ[0, p] + occ[0, q]
                top = twice[t * V : (t + 1) * V, s * V : (s + 1) * V]
                top = top - swapped[s * V : (s + 1) * V, t * V : (t + 1) * V]
                tiles.append((kept * top / ((total - va) - vb[...])).astype(jnp.bfloat16))
            columns.append(jnp.concatenate(tiles, axis=0))
        tilde = jnp.concatenate(columns, axis=1)
        qs.append(block)
        ts.append(tilde)
    gammas = jnp.dot(jnp.concatenate(qs, axis=1), jnp.concatenate(ts, axis=0), preferred_element_type=jnp.float32)
    for s in range(NP):
        gamma = jnp.where(live(p_index[s]), gammas[:, s * V : (s + 1) * V], 0.0) * (1 / SCALE)
        out[s] = gamma.reshape(16, 16, V)


def pair_terms(scalars, p_blocks, q_blocks):
    hbm = pl.BlockSpec(memory_space=pltpu.HBM)
    vmem = pl.BlockSpec(memory_space=pltpu.VMEM)
    return pl.pallas_call(
        pair_kernel,
        out_shape=jax.ShapeDtypeStruct((NP, 16, 16, V), jnp.float32),
        in_specs=[hbm] * 3 + [vmem] * 3,
        out_specs=vmem,
        scratch_shapes=[
            pltpu.VMEM((NA, NP * V), jnp.bfloat16),
            pltpu.VMEM((NP * V, NA), jnp.bfloat16),
            pltpu.VMEM((V, V), jnp.float32),
            pltpu.SMEM((2, NP * NZ), jnp.int32),
            pltpu.SMEM((NP * NZ, NP * NZ), jnp.int32),
            pltpu.SMEM((1, NP * NZ), jnp.float32),
            pltpu.SemaphoreType.DMA((3,)),
        ],
        compiler_params=pltpu.CompilerParams(vmem_limit_bytes=24 * 2**20),
        cost_estimate=pl.CostEstimate(flops=2 * 10**9, bytes_accessed=2 * 10**6, transcendentals=10**6),
    )(*scalars, p_blocks, q_blocks)


def on_device(b_tensor, significance, pair_keep, occ_energy, virt_energy):
    own = lax.all_to_all(b_tensor[0], AUX, 0, 0, tiled=True).reshape(1, NA, V)
    p_blocks = lax.all_to_all(jnp.broadcast_to(own, (NP, NA, V)), "blk_y", 0, 0, tiled=True)
    sent = (own.astype(jnp.float32) * SCALE).astype(jnp.float16)
    line = lax.all_gather(sent, "blk_z", axis=0, tiled=True)
    scalars = (significance[:, 0, :].T, pair_keep[0], occ_energy.T, virt_energy)
    part = pair_terms(scalars, p_blocks, line.astype(jnp.bfloat16))
    back = lax.all_to_all(part.reshape(32, 32, V), ("blk_y",) + AUX[:2], 0, 0, tiled=True)
    total = back.reshape(NP, 8, 2, 16, V).sum(axis=0)
    core = lax.axis_index("aux_core")
    got = lax.ppermute(jnp.where(core == 0, total[:, 1], total[:, 0]), "aux_core", [(0, 1), (1, 0)])
    place = lax.broadcasted_iota(jnp.int32, total.shape, 1)
    return jnp.where(place == core, total, got[:, None]).reshape(1, 16, 16, V)


def solution(mesh):
    blk = ("blk_y", "blk_z")
    fine = Mesh(mesh.devices.reshape(4, 2, 2, NP, NZ), AUX + blk)
    return jax.shard_map(
        on_device,
        mesh=fine,
        in_specs=(
            P(blk, None, AUX, None),
            P(None, AUX, None),
            P(AUX, None, None),
            P(None, AUX),
            P(AUX, None),
        ),
        out_specs=P(blk, None, AUX, None),
        check_vma=False,
    )
```

```python
import jax
import jax.numpy as jnp
from jax import lax
from jax.experimental import pallas as pl
from jax.experimental.pallas import tpu as pltpu
from jax.sharding import Mesh, PartitionSpec as P

AUX = ("aux_x", "aux_y", "aux_core")
NP = 4
NZ = 16
SCALE = 2.0**14
V = 128
AB = 128
NA = 256


def pair_kernel(sig_hbm, keep_hbm, occ_hbm, virt, p_ref, q_ref, out, here, pcat, pcat_t, vb, sig, keep, occ, done):
    copies = [
        pltpu.make_async_copy(src, dst, done.at[i])
        for i, (src, dst) in enumerate(((sig_hbm, sig), (keep_hbm, keep), (occ_hbm, occ)))
    ]
    for copy in copies:
        copy.start()
    va = virt[...]
    vb[...] = jnp.broadcast_to(va, (V, V)).T
    for copy in copies:
        copy.wait()
    h = lax.axis_index("blk_y")
    w = lax.axis_index("blk_z")
    rows = lax.broadcasted_iota(jnp.int32, (NA, V), 0)
    zero = jnp.zeros((NA, V), jnp.bfloat16)

    def live(orbital):
        return jnp.where(rows < AB, sig[0, orbital], sig[1, orbital]) > 0

    p_index = [s * NZ + w for s in range(NP)]
    for s in range(NP):
        block = jnp.where(live(p_index[s]), p_ref[s], zero) * (1 / SCALE)
        pcat[:, s * V : (s + 1) * V] = block * 2
        pcat_t[s * V : (s + 1) * V, :] = block.T
    place = lax.broadcasted_iota(jnp.int32, here.shape, 1)
    here[...] = (place == lax.axis_index("aux_core")).astype(jnp.int32)
    q_index = [h * NZ + k for k in range(NZ)]
    qs, ts = [], []
    for c in range(0, NZ, 2):
        block = jnp.concatenate([jnp.where(live(q_index[c + t]), q_ref[c + t], zero) for t in range(2)], axis=1)
        twice = jnp.dot(block.T, pcat[...], preferred_element_type=jnp.float32)
        swapped = jnp.dot(pcat_t[...], block, preferred_element_type=jnp.float32)
        columns = []
        for s in range(NP):
            tiles = []
            for t in range(2):
                p, q = p_index[s], q_index[c + t]
                kept = keep[lax.min(p, q), lax.max(p, q)].astype(jnp.float32)
                total = occ[0, p] + occ[0, q]
                top = twice[t * V : (t + 1) * V, s * V : (s + 1) * V]
                top = top - swapped[s * V : (s + 1) * V, t * V : (t + 1) * V]
                tiles.append((kept * top / ((total - va) - vb[...])).astype(jnp.bfloat16))
            columns.append(jnp.concatenate(tiles, axis=0))
        tilde = jnp.concatenate(columns, axis=1)
        qs.append(block)
        ts.append(tilde)
    gammas = jnp.dot(jnp.concatenate(qs, axis=1), jnp.concatenate(ts, axis=0), preferred_element_type=jnp.float32)
    for s in range(NP):
        gamma = jnp.where(live(p_index[s]), gammas[:, s * V : (s + 1) * V], 0.0) * (1 / SCALE)
        out[s] = gamma.reshape(16, 16, V)


def pair_terms(scalars, p_blocks, q_blocks):
    hbm = pl.BlockSpec(memory_space=pltpu.HBM)
    vmem = pl.BlockSpec(memory_space=pltpu.VMEM)
    return pl.pallas_call(
        pair_kernel,
        out_shape=(
            jax.ShapeDtypeStruct((NP, 16, 16, V), jnp.float32),
            jax.ShapeDtypeStruct((8, 2, 16, V), jnp.int32),
        ),
        in_specs=[hbm] * 3 + [vmem] * 3,
        out_specs=(vmem, vmem),
        scratch_shapes=[
            pltpu.VMEM((NA, NP * V), jnp.bfloat16),
            pltpu.VMEM((NP * V, NA), jnp.bfloat16),
            pltpu.VMEM((V, V), jnp.float32),
            pltpu.SMEM((2, NP * NZ), jnp.int32),
            pltpu.SMEM((NP * NZ, NP * NZ), jnp.int32),
            pltpu.SMEM((1, NP * NZ), jnp.float32),
            pltpu.SemaphoreType.DMA((3,)),
        ],
        compiler_params=pltpu.CompilerParams(vmem_limit_bytes=24 * 2**20),
        cost_estimate=pl.CostEstimate(flops=2 * 10**9, bytes_accessed=2 * 10**6, transcendentals=10**6),
    )(*scalars, p_blocks, q_blocks)


def on_device(b_tensor, significance, pair_keep, occ_energy, virt_energy):
    own = lax.all_to_all(b_tensor[0], AUX, 0, 0, tiled=True).reshape(1, NA, V)
    p_blocks = lax.all_to_all(jnp.broadcast_to(own, (NP, NA, V)), "blk_y", 0, 0, tiled=True)
    sent = (own.astype(jnp.float32) * SCALE).astype(jnp.float16)
    line = lax.all_gather(sent, "blk_z", axis=0, tiled=True)
    scalars = (significance[:, 0, :].T, pair_keep[0], occ_energy.T, virt_energy)
    part, here = pair_terms(scalars, p_blocks, line.astype(jnp.bfloat16))
    back = lax.all_to_all(part.reshape(32, 32, V), ("blk_y",) + AUX[:2], 0, 0, tiled=True)
    total = back.reshape(NP, 8, 2, 16, V).sum(axis=0)
    got = lax.ppermute(jnp.where(here[:, 0] > 0, total[:, 1], total[:, 0]), "aux_core", [(0, 1), (1, 0)])
    return jnp.where(here > 0, total, got[:, None]).reshape(1, 16, 16, V)


def solution(mesh):
    blk = ("blk_y", "blk_z")
    fine = Mesh(mesh.devices.reshape(4, 2, 2, NP, NZ), AUX + blk)
    return jax.shard_map(
        on_device,
        mesh=fine,
        in_specs=(
            P(blk, None, AUX, None),
            P(None, AUX, None),
            P(AUX, None, None),
            P(None, AUX),
            P(AUX, None),
        ),
        out_specs=P(blk, None, AUX, None),
        check_vma=False,
    )
```

```python
import jax
import jax.numpy as jnp
from jax import lax
from jax.experimental import pallas as pl
from jax.experimental.pallas import tpu as pltpu
from jax.sharding import Mesh, PartitionSpec as P

AUX = ("aux_x", "aux_y", "aux_core")
NP = 4
NZ = 16
SCALE = 2.0**14
V = 128
AB = 128
NA = 256


def pair_kernel(sig_hbm, keep_hbm, occ_hbm, virt, p0, p1, p2, p3, q_ref, out, here, pcat, pcat_t, vb, sig, keep, occ, done):
    copies = [
        pltpu.make_async_copy(src, dst, done.at[i])
        for i, (src, dst) in enumerate(((sig_hbm, sig), (keep_hbm, keep), (occ_hbm, occ)))
    ]
    for copy in copies:
        copy.start()
    va = virt[...]
    vb[...] = jnp.broadcast_to(va, (V, V)).T
    for copy in copies:
        copy.wait()
    h = lax.axis_index("blk_y")
    w = lax.axis_index("blk_z")
    rows = lax.broadcasted_iota(jnp.int32, (NA, V), 0)
    zero = jnp.zeros((NA, V), jnp.bfloat16)

    def live(orbital):
        return jnp.where(rows < AB, sig[0, orbital], sig[1, orbital]) > 0

    p_index = [lax.rem(h + s, NP) * NZ + w for s in range(NP)]
    for s in range(NP):
        block = jnp.where(live(p_index[s]), (p0, p1, p2, p3)[s][0], zero) * (1 / SCALE)
        pcat[:, s * V : (s + 1) * V] = block * 2
        pcat_t[s * V : (s + 1) * V, :] = block.T
    place = lax.broadcasted_iota(jnp.int32, here.shape, 1)
    here[...] = (place == lax.axis_index("aux_core")).astype(jnp.int32)
    q_index = [h * NZ + k for k in range(NZ)]
    qs, ts = [], []
    for c in range(0, NZ, 2):
        block = jnp.concatenate([jnp.where(live(q_index[c + t]), q_ref[c + t], zero) for t in range(2)], axis=1)
        twice = jnp.dot(block.T, pcat[...], preferred_element_type=jnp.float32)
        swapped = jnp.dot(pcat_t[...], block, preferred_element_type=jnp.float32)
        columns = []
        for s in range(NP):
            tiles = []
            for t in range(2):
                p, q = p_index[s], q_index[c + t]
                kept = keep[lax.min(p, q), lax.max(p, q)].astype(jnp.float32)
                total = occ[0, p] + occ[0, q]
                top = twice[t * V : (t + 1) * V, s * V : (s + 1) * V]
                top = top - swapped[s * V : (s + 1) * V, t * V : (t + 1) * V]
                tiles.append((kept * top / ((total - va) - vb[...])).astype(jnp.bfloat16))
            columns.append(jnp.concatenate(tiles, axis=0))
        tilde = jnp.concatenate(columns, axis=1)
        qs.append(block)
        ts.append(tilde)
    gammas = jnp.dot(jnp.concatenate(qs, axis=1), jnp.concatenate(ts, axis=0), preferred_element_type=jnp.float32)
    for s in range(NP):
        gamma = jnp.where(live(p_index[s]), gammas[:, s * V : (s + 1) * V], 0.0) * (1 / SCALE)
        out[lax.rem(h + s, NP)] = gamma.reshape(16, 16, V)


def pair_terms(scalars, p_blocks, q_blocks):
    hbm = pl.BlockSpec(memory_space=pltpu.HBM)
    vmem = pl.BlockSpec(memory_space=pltpu.VMEM)
    return pl.pallas_call(
        pair_kernel,
        out_shape=(
            jax.ShapeDtypeStruct((NP, 16, 16, V), jnp.float32),
            jax.ShapeDtypeStruct((8, 2, 16, V), jnp.int32),
        ),
        in_specs=[hbm] * 3 + [vmem] * (2 + NP),
        out_specs=(vmem, vmem),
        scratch_shapes=[
            pltpu.VMEM((NA, NP * V), jnp.bfloat16),
            pltpu.VMEM((NP * V, NA), jnp.bfloat16),
            pltpu.VMEM((V, V), jnp.float32),
            pltpu.SMEM((2, NP * NZ), jnp.int32),
            pltpu.SMEM((NP * NZ, NP * NZ), jnp.int32),
            pltpu.SMEM((1, NP * NZ), jnp.float32),
            pltpu.SemaphoreType.DMA((3,)),
        ],
        compiler_params=pltpu.CompilerParams(vmem_limit_bytes=24 * 2**20),
        cost_estimate=pl.CostEstimate(flops=2 * 10**9, bytes_accessed=2 * 10**6, transcendentals=10**6),
    )(*scalars, *p_blocks, q_blocks)


def on_device(b_tensor, significance, pair_keep, occ_energy, virt_energy):
    own = lax.all_to_all(b_tensor[0], AUX, 0, 0, tiled=True).reshape(1, NA, V)
    p_blocks = [own] + [lax.ppermute(own, "blk_y", [((i + s) % NP, i) for i in range(NP)]) for s in range(1, NP)]
    sent = (own.astype(jnp.float32) * SCALE).astype(jnp.float16)
    line = lax.all_gather(sent, "blk_z", axis=0, tiled=True)
    scalars = (significance[:, 0, :].T, pair_keep[0], occ_energy.T, virt_energy)
    part, here = pair_terms(scalars, p_blocks, line.astype(jnp.bfloat16))
    back = lax.all_to_all(part.reshape(32, 32, V), ("blk_y",) + AUX[:2], 0, 0, tiled=True)
    total = back.reshape(NP, 8, 2, 16, V).sum(axis=0)
    got = lax.ppermute(jnp.where(here[:, 0] > 0, total[:, 1], total[:, 0]), "aux_core", [(0, 1), (1, 0)])
    return jnp.where(here > 0, total, got[:, None]).reshape(1, 16, 16, V)


def solution(mesh):
    blk = ("blk_y", "blk_z")
    fine = Mesh(mesh.devices.reshape(4, 2, 2, NP, NZ), AUX + blk)
    return jax.shard_map(
        on_device,
        mesh=fine,
        in_specs=(
            P(blk, None, AUX, None),
            P(None, AUX, None),
            P(AUX, None, None),
            P(None, AUX),
            P(AUX, None),
        ),
        out_specs=P(blk, None, AUX, None),
        check_vma=False,
    )
```

```python
import jax
import jax.numpy as jnp
from jax import lax
from jax.experimental import pallas as pl
from jax.experimental.pallas import tpu as pltpu
from jax.sharding import Mesh, PartitionSpec as P

AUX = ("aux_x", "aux_y", "aux_core")
NP = 4
NZ = 16
SCALE = 2.0**14
V = 128
AB = 128
NA = 256


def pair_kernel(sig_hbm, keep_hbm, occ_hbm, virt, p_ref, q_ref, out, here, pcat, pcat_t, vb, sig, keep, occ, done):
    copies = [
        pltpu.make_async_copy(src, dst, done.at[i])
        for i, (src, dst) in enumerate(((sig_hbm, sig), (keep_hbm, keep), (occ_hbm, occ)))
    ]
    for copy in copies:
        copy.start()
    va = virt[...]
    vb[...] = jnp.broadcast_to(va, (V, V)).T
    for copy in copies:
        copy.wait()
    h = lax.axis_index("blk_y")
    w = lax.axis_index("blk_z")
    rows = lax.broadcasted_iota(jnp.int32, (NA, V), 0)
    zero = jnp.zeros((NA, V), jnp.bfloat16)

    def live(orbital):
        return jnp.where(rows < AB, sig[0, orbital], sig[1, orbital]) > 0

    p_index = [s * NZ + w for s in range(NP)]
    for s in range(NP):
        block = jnp.where(live(p_index[s]), p_ref[s], zero) * (1 / SCALE)
        pcat[:, s * V : (s + 1) * V] = block * 2
        pcat_t[s * V : (s + 1) * V, :] = block.T
    place = lax.broadcasted_iota(jnp.int32, here.shape, 1)
    here[...] = (place == lax.axis_index("aux_core")).astype(jnp.int32)
    q_index = [h * NZ + k for k in range(NZ)]
    qs, ts = [], []
    for c in range(0, NZ, 2):
        block = jnp.concatenate([jnp.where(live(q_index[c + t]), q_ref[c + t], zero) for t in range(2)], axis=1)
        twice = jnp.dot(block.T, pcat[...], preferred_element_type=jnp.float32)
        swapped = jnp.dot(pcat_t[...], block, preferred_element_type=jnp.float32)
        columns = []
        for s in range(NP):
            tiles = []
            for t in range(2):
                p, q = p_index[s], q_index[c + t]
                kept = keep[lax.min(p, q), lax.max(p, q)]
                total = occ[0, p] + occ[0, q]
                top = twice[t * V : (t + 1) * V, s * V : (s + 1) * V]
                top = top - swapped[s * V : (s + 1) * V, t * V : (t + 1) * V]
                tiles.append((kept * top / ((va - total) + vb[...])).astype(jnp.bfloat16))
            columns.append(jnp.concatenate(tiles, axis=0))
        tilde = jnp.concatenate(columns, axis=1)
        qs.append(block)
        ts.append(tilde)
    gammas = jnp.dot(jnp.concatenate(qs, axis=1), jnp.concatenate(ts, axis=0), preferred_element_type=jnp.float32)
    for s in range(NP):
        gamma = jnp.where(live(p_index[s]), gammas[:, s * V : (s + 1) * V], 0.0) * (1 / SCALE)
        out[s] = gamma.reshape(16, 16, V)


def pair_terms(scalars, p_blocks, q_blocks):
    hbm = pl.BlockSpec(memory_space=pltpu.HBM)
    vmem = pl.BlockSpec(memory_space=pltpu.VMEM)
    return pl.pallas_call(
        pair_kernel,
        out_shape=(
            jax.ShapeDtypeStruct((NP, 16, 16, V), jnp.float32),
            jax.ShapeDtypeStruct((8, 2, 16, V), jnp.int32),
        ),
        in_specs=[hbm] * 3 + [vmem] * 3,
        out_specs=(vmem, vmem),
        scratch_shapes=[
            pltpu.VMEM((NA, NP * V), jnp.bfloat16),
            pltpu.VMEM((NP * V, NA), jnp.bfloat16),
            pltpu.VMEM((V, V), jnp.float32),
            pltpu.SMEM((2, NP * NZ), jnp.float32),
            pltpu.SMEM((NP * NZ, NP * NZ), jnp.float32),
            pltpu.SMEM((1, NP * NZ), jnp.float32),
            pltpu.SemaphoreType.DMA((3,)),
        ],
        compiler_params=pltpu.CompilerParams(vmem_limit_bytes=24 * 2**20),
        cost_estimate=pl.CostEstimate(flops=2 * 10**9, bytes_accessed=2 * 10**6, transcendentals=10**6),
    )(*scalars, p_blocks, q_blocks)


def on_device(b_tensor, significance, pair_keep, occ_energy, virt_energy):
    own = lax.all_to_all(b_tensor[0], AUX, 0, 0, tiled=True).reshape(1, NA, V)
    p_blocks = lax.all_to_all(jnp.broadcast_to(own, (NP, NA, V)), "blk_y", 0, 0, tiled=True)
    sent = (own.astype(jnp.float32) * SCALE).astype(jnp.float16)
    scalars = (
        significance[:, 0, :].T.astype(jnp.float32),
        pair_keep[0].astype(jnp.float32),
        -occ_energy.T,
        -virt_energy,
    )
    sent, *scalars = lax.optimization_barrier((sent, *scalars))
    line = lax.all_gather(sent, "blk_z", axis=0, tiled=True)
    part, here = pair_terms(scalars, p_blocks, line.astype(jnp.bfloat16))
    back = lax.all_to_all(part.reshape(32, 32, V), ("blk_y",) + AUX[:2], 0, 0, tiled=True)
    total = back.reshape(NP, 8, 2, 16, V).sum(axis=0)
    got = lax.ppermute(jnp.where(here[:, 0] > 0, total[:, 1], total[:, 0]), "aux_core", [(0, 1), (1, 0)])
    return jnp.where(here > 0, total, got[:, None]).reshape(1, 16, 16, V)


def solution(mesh):
    blk = ("blk_y", "blk_z")
    fine = Mesh(mesh.devices.reshape(4, 2, 2, NP, NZ), AUX + blk)
    return jax.shard_map(
        on_device,
        mesh=fine,
        in_specs=(
            P(blk, None, AUX, None),
            P(None, AUX, None),
            P(AUX, None, None),
            P(None, AUX),
            P(AUX, None),
        ),
        out_specs=P(blk, None, AUX, None),
        check_vma=False,
    )
```

```python
import jax
import jax.numpy as jnp
from jax import lax
from jax.experimental import pallas as pl
from jax.experimental.pallas import tpu as pltpu
from jax.sharding import Mesh, PartitionSpec as P

AUX = ("aux_x", "aux_y", "aux_core")
NP = 4
NZ = 16
SCALE = 2.0**14
V = 128
AB = 128
NA = 256


def pair_kernel(sig_hbm, keep_hbm, occ_hbm, virt, p_ref, q_ref, out, here, pcat, pcat_t, vb, sig, keep, occ, done):
    copies = [
        pltpu.make_async_copy(src, dst, done.at[i])
        for i, (src, dst) in enumerate(((sig_hbm, sig), (keep_hbm, keep), (occ_hbm, occ)))
    ]
    for copy in copies:
        copy.start()
    va = virt[...]
    vb[...] = jnp.broadcast_to(va, (V, V)).T
    for copy in copies:
        copy.wait()
    h = lax.axis_index("blk_y")
    w = lax.axis_index("blk_z")
    rows = lax.broadcasted_iota(jnp.int32, (NA, V), 0)
    zero = jnp.zeros((NA, V), jnp.bfloat16)

    def live(orbital):
        return jnp.where(rows < AB, sig[0, orbital], sig[1, orbital]) > 0

    p_index = [s * NZ + w for s in range(NP)]
    for s in range(NP):
        block = jnp.where(live(p_index[s]), p_ref[s], zero) * (1 / SCALE)
        pcat[:, s * V : (s + 1) * V] = block * 2
        pcat_t[s * V : (s + 1) * V, :] = block.T
    place = lax.broadcasted_iota(jnp.int32, here.shape, 1)
    here[...] = (place == lax.axis_index("aux_core")).astype(jnp.int32)
    q_index = [h * NZ + k for k in range(NZ)]
    qs, ts = [], []
    for c in range(0, NZ, 2):
        block = jnp.concatenate([jnp.where(live(q_index[c + t]), q_ref[c + t], zero) for t in range(2)], axis=1)
        twice = jnp.dot(block.T, pcat[...], preferred_element_type=jnp.float32)
        swapped = jnp.dot(pcat_t[...], block, preferred_element_type=jnp.float32)
        columns = []
        for s in range(NP):
            tiles = []
            for t in range(2):
                p, q = p_index[s], q_index[c + t]
                kept = keep[lax.min(p, q), lax.max(p, q)]
                total = occ[0, p] + occ[0, q]
                top = twice[t * V : (t + 1) * V, s * V : (s + 1) * V]
                top = top - swapped[s * V : (s + 1) * V, t * V : (t + 1) * V]
                tiles.append((kept * top / ((va - total) + vb[...])).astype(jnp.bfloat16))
            columns.append(jnp.concatenate(tiles, axis=0))
        tilde = jnp.concatenate(columns, axis=1)
        qs.append(block)
        ts.append(tilde)
    gammas = jnp.dot(jnp.concatenate(qs, axis=1), jnp.concatenate(ts, axis=0), preferred_element_type=jnp.float32)
    for s in range(NP):
        gamma = jnp.where(live(p_index[s]), gammas[:, s * V : (s + 1) * V], 0.0) * (1 / SCALE)
        out[s] = gamma.reshape(16, 16, V)


def pair_terms(scalars, p_blocks, q_blocks):
    hbm = pl.BlockSpec(memory_space=pltpu.HBM)
    vmem = pl.BlockSpec(memory_space=pltpu.VMEM)
    return pl.pallas_call(
        pair_kernel,
        out_shape=(
            jax.ShapeDtypeStruct((NP, 16, 16, V), jnp.float32),
            jax.ShapeDtypeStruct((8, 2, 16, V), jnp.int32),
        ),
        in_specs=[hbm] * 3 + [vmem] * 3,
        out_specs=(vmem, vmem),
        scratch_shapes=[
            pltpu.VMEM((NA, NP * V), jnp.bfloat16),
            pltpu.VMEM((NP * V, NA), jnp.bfloat16),
            pltpu.VMEM((V, V), jnp.float32),
            pltpu.SMEM((2, NP * NZ), jnp.float32),
            pltpu.SMEM((NP * NZ, NP * NZ), jnp.float32),
            pltpu.SMEM((1, NP * NZ), jnp.float32),
            pltpu.SemaphoreType.DMA((3,)),
        ],
        compiler_params=pltpu.CompilerParams(vmem_limit_bytes=24 * 2**20),
        cost_estimate=pl.CostEstimate(flops=2 * 10**9, bytes_accessed=2 * 10**6, transcendentals=10**6),
    )(*scalars, p_blocks, q_blocks)


def on_device(b_tensor, significance, pair_keep, occ_energy, virt_energy):
    own = lax.all_to_all(b_tensor[0], AUX, 0, 0, tiled=True).reshape(1, NA, V)
    p_blocks = lax.all_to_all(jnp.broadcast_to(own, (NP, NA, V)), "blk_y", 0, 0, tiled=True)
    sent = (own.astype(jnp.float32) * SCALE).astype(jnp.float16)
    scalars = (
        significance[:, 0, :].T.astype(jnp.float32),
        pair_keep[0].astype(jnp.float32),
        -occ_energy.T,
        -virt_energy,
    )
    sent, *scalars = lax.optimization_barrier((sent, *scalars))
    line = lax.all_gather(sent, "blk_z", axis=0, tiled=True)
    part, here = pair_terms(scalars, p_blocks, line.astype(jnp.bfloat16))
    back = lax.all_to_all(part.reshape(NP, NA, V), "blk_y", 0, 0, tiled=True).sum(axis=0)
    total = lax.all_to_all(back.reshape(8, 32, V), AUX[:2], 0, 0, tiled=True).reshape(8, 2, 16, V)
    got = lax.ppermute(jnp.where(here[:, 0] > 0, total[:, 1], total[:, 0]), "aux_core", [(0, 1), (1, 0)])
    return jnp.where(here > 0, total, got[:, None]).reshape(1, 16, 16, V)


def solution(mesh):
    blk = ("blk_y", "blk_z")
    fine = Mesh(mesh.devices.reshape(4, 2, 2, NP, NZ), AUX + blk)
    return jax.shard_map(
        on_device,
        mesh=fine,
        in_specs=(
            P(blk, None, AUX, None),
            P(None, AUX, None),
            P(AUX, None, None),
            P(None, AUX),
            P(AUX, None),
        ),
        out_specs=P(blk, None, AUX, None),
        check_vma=False,
    )
```

```python
import jax
import jax.numpy as jnp
from jax import lax
from jax.experimental import pallas as pl
from jax.experimental.pallas import tpu as pltpu
from jax.sharding import Mesh, PartitionSpec as P

AUX = ("aux_x", "aux_y", "aux_core")
NP = 4
NZ = 16
RINGS = [list(range(NZ)), list(range(2 * NZ - 1, NZ - 1, -1))]
SCALE = 2.0**14
V = 128
AB = 128
NA = 256


def pair_kernel(sig_hbm, keep_hbm, occ_hbm, virt, p_ref, q_ref, out, here, pcat, pcat_t, vb, sig, keep, occ, done):
    copies = [
        pltpu.make_async_copy(src, dst, done.at[i])
        for i, (src, dst) in enumerate(((sig_hbm, sig), (keep_hbm, keep), (occ_hbm, occ)))
    ]
    for copy in copies:
        copy.start()
    va = virt[...]
    vb[...] = jnp.broadcast_to(va, (V, V)).T
    copies[0].wait()
    h = lax.axis_index("blk_y")
    w = lax.axis_index("blk_z")
    rows = lax.broadcasted_iota(jnp.int32, (NA, V), 0)
    zero = jnp.zeros((NA, V), jnp.bfloat16)

    def live(orbital):
        return jnp.where(rows < AB, sig[0, orbital], sig[1, orbital]) > 0

    p_index = [s * NZ + w for s in range(NP)]
    for s in range(NP):
        block = jnp.where(live(p_index[s]), p_ref[s], zero) * (1 / SCALE)
        pcat[:, s * V : (s + 1) * V] = block * 2
        pcat_t[s * V : (s + 1) * V, :] = block.T
    place = lax.broadcasted_iota(jnp.int32, here.shape, 1)
    here[...] = (place == lax.axis_index("aux_core")).astype(jnp.int32)
    copies[1].wait()
    copies[2].wait()
    core = lax.axis_index("aux_core")
    q_index = [h * NZ + jnp.where(core == 0, k, NZ - 1 - k) for k in range(NZ)]
    qs, ts = [], []
    for c in range(0, NZ, 2):
        block = jnp.concatenate([jnp.where(live(q_index[c + t]), q_ref[c + t], zero) for t in range(2)], axis=1)
        twice = jnp.dot(block.T, pcat[...], preferred_element_type=jnp.float32)
        swapped = jnp.dot(pcat_t[...], block, preferred_element_type=jnp.float32)
        columns = []
        for s in range(NP):
            tiles = []
            for t in range(2):
                p, q = p_index[s], q_index[c + t]
                kept = keep[lax.min(p, q), lax.max(p, q)]
                total = occ[0, p] + occ[0, q]
                top = twice[t * V : (t + 1) * V, s * V : (s + 1) * V]
                top = top - swapped[s * V : (s + 1) * V, t * V : (t + 1) * V]
                tiles.append((kept * top / ((va - total) + vb[...])).astype(jnp.bfloat16))
            columns.append(jnp.concatenate(tiles, axis=0))
        tilde = jnp.concatenate(columns, axis=1)
        qs.append(block)
        ts.append(tilde)
    gammas = jnp.dot(jnp.concatenate(qs, axis=1), jnp.concatenate(ts, axis=0), preferred_element_type=jnp.float32)
    for s in range(NP):
        gamma = jnp.where(live(p_index[s]), gammas[:, s * V : (s + 1) * V], 0.0) * (1 / SCALE)
        out[s] = gamma.reshape(16, 16, V)


def pair_terms(scalars, p_blocks, q_blocks):
    hbm = pl.BlockSpec(memory_space=pltpu.HBM)
    vmem = pl.BlockSpec(memory_space=pltpu.VMEM)
    return pl.pallas_call(
        pair_kernel,
        out_shape=(
            jax.ShapeDtypeStruct((NP, 16, 16, V), jnp.float32),
            jax.ShapeDtypeStruct((8, 2, 16, V), jnp.int32),
        ),
        in_specs=[hbm] * 3 + [vmem] * 3,
        out_specs=(vmem, vmem),
        scratch_shapes=[
            pltpu.VMEM((NA, NP * V), jnp.bfloat16),
            pltpu.VMEM((NP * V, NA), jnp.bfloat16),
            pltpu.VMEM((V, V), jnp.float32),
            pltpu.SMEM((2, NP * NZ), jnp.float32),
            pltpu.SMEM((NP * NZ, NP * NZ), jnp.float32),
            pltpu.SMEM((1, NP * NZ), jnp.float32),
            pltpu.SemaphoreType.DMA((3,)),
        ],
        compiler_params=pltpu.CompilerParams(vmem_limit_bytes=24 * 2**20),
        cost_estimate=pl.CostEstimate(flops=2 * 10**9, bytes_accessed=2 * 10**6, transcendentals=10**6),
    )(*scalars, p_blocks, q_blocks)


def on_device(b_tensor, significance, pair_keep, occ_energy, virt_energy):
    own = lax.all_to_all(b_tensor[0], AUX, 0, 0, tiled=True).reshape(1, NA, V)
    p_blocks = lax.all_to_all(jnp.broadcast_to(own, (NP, NA, V)), "blk_y", 0, 0, tiled=True)
    sent = (own.astype(jnp.float32) * SCALE).astype(jnp.float16)
    scalars = (
        significance[:, 0, :].T.astype(jnp.float32),
        pair_keep[0].astype(jnp.float32),
        -occ_energy.T,
        -virt_energy,
    )
    sent, *scalars = lax.optimization_barrier((sent, *scalars))
    line = lax.all_gather(sent, ("aux_core", "blk_z"), axis=0, tiled=True, axis_index_groups=RINGS)
    part, here = pair_terms(scalars, p_blocks, line.astype(jnp.bfloat16))
    back = lax.all_to_all(part.reshape(32, 32, V), ("blk_y",) + AUX[:2], 0, 0, tiled=True)
    total = back.reshape(NP, 8, 2, 16, V).sum(axis=0)
    got = lax.ppermute(jnp.where(here[:, 0] > 0, total[:, 1], total[:, 0]), "aux_core", [(0, 1), (1, 0)])
    return jnp.where(here > 0, total, got[:, None]).reshape(1, 16, 16, V)


def solution(mesh):
    blk = ("blk_y", "blk_z")
    fine = Mesh(mesh.devices.reshape(4, 2, 2, NP, NZ), AUX + blk)
    return jax.shard_map(
        on_device,
        mesh=fine,
        in_specs=(
            P(blk, None, AUX, None),
            P(None, AUX, None),
            P(AUX, None, None),
            P(None, AUX),
            P(AUX, None),
        ),
        out_specs=P(blk, None, AUX, None),
        check_vma=False,
    )
```
